256 devices in a mesh: gr: 32 (over x_lo, z, core), gc: 8 (over y, x_hi).
Axes of the slice: x: 4 (x_hi: 2, x_lo: 2; x = x_hi * 2 + x_lo), y: 4, z: 8, core: 2. Of those that a mesh axis runs over, the one named last changes fastest.
Arguments:
- tile_counts: int32 [32, 8, 1024, 1024], P('gr', 'gc'), may hold values from 0 to 4095, as said below
- row_slot: int32 [32, 8, 1024], P('gr', 'gc'), may hold values from 0 to 1023, each once within a row
- col_slot: int32 [32, 8, 1024], P('gr', 'gc'), may hold values from 0 to 1023, each once within a row
- row_embed: float32 [32, 1024, 256], P('gr', 'gc'), may hold values from -2 to 2
- col_embed: float32 [8, 1024, 256], P('gc', 'gr'), may hold values from -2 to 2
- row_marginal: int32 [32, 1024], P('gr', 'gc'), may hold values from 30 to 2999
- col_marginal: int32 [8, 1024], P('gc', 'gr'), may hold values from 30 to 2999
- total_count: int32 [1], replicated, may hold values from 1048576 to 16777215
Outputs:
- new_rows: float32 [32, 1024, 256], P('gr', 'gc')
- new_cols: float32 [8, 1024, 256], P('gc', 'gr')
The draws below stay inside these ranges and needn't reach their ends.
Inputs may be any that keep to these rules, and one draw needn't show every extreme that they name: `tile_counts`: each tile's counts, 0 for pairs never seen. `row_slot`: each tile's row slots name every block row once. `col_slot`: each tile's column slots name every block column once.
All inputs are finite; a program needn't handle non-finite values.
Results may differ from the reference program's by a relative error of at most 0.0003.
Values sent between devices are 32-bit elements; how exact they have to be, the bound alone decides.
No kernel may reach another device: no remote copies, remote signals or barrier semaphores. Data moves between devices by JAX's collectives and lax.ppermute only.
A program may use at most 64 MiB of HBM per device.

```python
import jax
import jax.numpy as jnp
from jax import lax

D = 256
ROWS = 1024
COLS = 1024
N_GR = 32
N_GC = 8


def draw_tile_counts(key, part):
    key = jax.random.fold_in(key, 5)
    first, second, third = jax.random.split(key, 3)
    shape = (N_GR, N_GC, ROWS, COLS)
    level = jax.random.randint(first, shape, 0, 12)
    width = jnp.left_shift(jnp.ones(shape, jnp.int32), level)
    extra = jax.random.randint(second, shape, 0, width)
    keep = jax.random.randint(third, shape, 0, 5) >= 2
    return jnp.where(keep, width + extra, 0).astype(jnp.int32)


def with_ends(array, own_key, low, high):
    extent = array.shape
    place = [jax.random.randint(jax.random.fold_in(own_key, axis), (), 0, extent[axis]) for axis in range(len(extent))]
    array = array.at[tuple(place)].set(low)
    longest = extent.index(max(extent))
    place[longest] = (place[longest] + 1) % extent[longest]
    return array.at[tuple(place)].set(high)


def shard_levels(key, extent, cuts, low, largest):
    factor_of, own = 1.0, jax.random.fold_in(key, 6)
    for position, parts in cuts:
        draws = jnp.exp(jax.random.uniform(jax.random.fold_in(own, position), (parts,), jnp.float32, low / len(cuts), largest / len(cuts)))
        factor_of = factor_of * jnp.repeat(draws, extent[position] // parts).reshape([-1 if axis == position else 1 for axis in range(len(extent))])
    return factor_of


def normal_values(rng, shape, deviation, bound, cuts=(), kind=jnp.bfloat16):
    entries = jax.random.normal(rng, shape, jnp.float32) * deviation
    if len(cuts) > 0:
        entries = shard_levels(rng, shape, cuts, -0.22, 0.18) * entries
    return jnp.clip(entries, min=-bound, max=bound).astype(kind)


def setup_inputs(seed: int = 0) -> dict:
    keys = jax.random.split(jax.random.key(seed), 9)
    tile_counts = draw_tile_counts(jax.random.fold_in(keys[8], 71), 0)
    row_slot = jax.vmap(lambda own: jax.random.permutation(own, ROWS))(jax.random.split(keys[1], N_GR * N_GC)).reshape((N_GR, N_GC, ROWS)).astype(jnp.int32)
    col_slot = jax.vmap(lambda own: jax.random.permutation(own, COLS))(jax.random.split(keys[2], N_GR * N_GC)).reshape((N_GR, N_GC, COLS)).astype(jnp.int32)
    row_embed = normal_values(keys[3], (N_GR, ROWS, D), 0.33, 2.0, ((0, 32), (1, 8)), jnp.float32)
    col_embed = normal_values(keys[4], (N_GC, COLS, D), 0.33, 2.0, ((0, 8), (1, 32)), jnp.float32)
    row_marginal = with_ends(jax.random.randint(keys[5], (N_GR, ROWS), 30, 3000), jax.random.fold_in(keys[5], 1), 30, 2999).astype(jnp.int32)
    col_marginal = with_ends(jax.random.randint(keys[6], (N_GC, COLS), 30, 3000), jax.random.fold_in(keys[6], 1), 30, 2999).astype(jnp.int32)
    total_count = jax.random.randint(keys[7], (1,), 1048576, 16777216).astype(jnp.int32)
    return dict(tile_counts=tile_counts, row_slot=row_slot, col_slot=col_slot, row_embed=row_embed, col_embed=col_embed, row_marginal=row_marginal, col_marginal=col_marginal, total_count=total_count)


def cell_gradient(score, counts, base):
    weight = counts.astype(jnp.float32)
    pmi = base + jnp.log(jnp.maximum(weight, 1.0))
    diff = score - pmi
    return jnp.where(counts > 0, (0.1 + 0.25 * jnp.sqrt(weight)) * diff, jax.nn.sigmoid(diff))

def reference(tile_counts, row_slot, col_slot, row_embed, col_embed, row_marginal, col_marginal, total_count):
    log_total = jnp.log(total_count.astype(jnp.float32))[0]
    log_rows = jnp.log(row_marginal.astype(jnp.float32))
    log_cols = jnp.log(col_marginal.astype(jnp.float32))
    row_iota = jnp.arange(ROWS, dtype=jnp.int32)
    col_iota = jnp.arange(COLS, dtype=jnp.int32)

    def one_tile(carry, index):
        row_total, col_total = carry
        rblock = index // N_GC
        cblock = index % N_GC
        inv_rows = jnp.zeros((ROWS,), jnp.int32).at[row_slot[rblock, cblock]].set(row_iota)
        inv_cols = jnp.zeros((COLS,), jnp.int32).at[col_slot[rblock, cblock]].set(col_iota)
        counts = tile_counts[rblock, cblock][inv_rows][:, inv_cols]
        left = row_embed[rblock]
        right = col_embed[cblock]
        base = log_total - log_rows[rblock][:, None] - log_cols[cblock][None, :]
        score = jnp.dot(left, right.T, precision=lax.Precision.HIGHEST)
        grads = cell_gradient(score, counts, base)
        row_term = jnp.dot(grads, right, precision=lax.Precision.HIGHEST)
        col_term = jnp.dot(grads.T, left, precision=lax.Precision.HIGHEST)
        row_total = row_total.at[rblock].add(row_term)
        col_total = col_total.at[cblock].add(col_term)
        return ((row_total, col_total), None)
    start = (jnp.zeros((N_GR, ROWS, D), jnp.float32), jnp.zeros((N_GC, COLS, D), jnp.float32))
    (row_grad, col_grad), unused = lax.scan(one_tile, start, jnp.arange(N_GR * N_GC, dtype=jnp.int32))
    return (row_embed - 0.001 * row_grad, col_embed - 0.001 * col_grad)
```

```python
import functools

import jax
import jax.numpy as jnp
from jax import lax
from jax.experimental import pallas as pl
from jax.experimental.pallas import tpu as pltpu
from jax.sharding import PartitionSpec as P

F32 = jnp.float32
BF16 = jnp.bfloat16
N = 1024
D = 256
NN = ((1,), (0,))
NT = ((1,), (1,))
VMEM = pl.BlockSpec(memory_space=pltpu.VMEM)
SMEM = pl.BlockSpec(memory_space=pltpu.SMEM)


def dot(a, b, dims):
    return lax.dot_general(a, b, (dims, ((), ())), preferred_element_type=F32)


def split(v):
    hi = v.astype(BF16)
    return hi, (v - hi.astype(F32)).astype(BF16)


def shift(x, axis, k):
    if axis == "gc":
        pairs = [(i, (i + k) % 8) for i in range(8)]
        return lax.ppermute(x, "gc", pairs)
    pairs = [(i, (i & 17) | (((((i >> 1) & 7) + k) % 8) << 1)) for i in range(32)]
    return lax.ppermute(x, "gr", pairs)


def swap(x, mask):
    return lax.ppermute(x, "gr", [(i, i ^ mask) for i in range(32)])


def prep_body(pos, cnt, rs, cs, w, lx, chi, clo, bt):
    gc, gr = pos[0], pos[1]
    rows = rs[...]
    rows = (((gc - (rows >> 7)) & 7) << 7) | (rows & 127)
    cols = cs[...]
    owner = cols >> 5
    cols = (
        (((owner ^ gr) & 1) << 9)
        | ((((gr >> 1) - (owner >> 1)) & 7) << 6)
        | (((owner ^ gr) & 16) << 1)
        | (cols & 31)
    )
    T = 256

    def load(t, _):
        s = pl.ds(pl.multiple_of(t * T, T), T)
        c = cnt[s, :]
        hi = c >> 6
        chi[s, :] = hi.astype(F32).astype(BF16)
        clo[s, :] = (c & 63).astype(F32).astype(BF16)
        j = lax.broadcasted_iota(jnp.int32, (T, N), 0) + t * T
        bt[s, :] = jnp.where(j == cols, 1.0, 0.0).astype(BF16)
        return 0

    lax.fori_loop(0, N // T, load, 0)

    def step(t, _):
        s = pl.ds(pl.multiple_of(t * T, T), T)
        i = lax.broadcasted_iota(jnp.int32, (T, N), 0) + t * T
        a = jnp.where(i == rows, 1.0, 0.0).astype(BF16)
        hi = dot(a, chi[...], NN).astype(BF16)
        lo = dot(a, clo[...], NN).astype(BF16)
        x = dot(hi, bt[...], NT) * 64.0 + dot(lo, bt[...], NT)
        w[s, :] = jnp.where(x > 0, 0.1 + 0.25 * jnp.sqrt(x), 0.0)
        lx[s, :] = jnp.log(jnp.maximum(x, 1.0))
        return 0

    lax.fori_loop(0, N // T, step, 0)


def prep(pos, cnt, rs, cs):
    return pl.pallas_call(
        prep_body,
        out_shape=[jax.ShapeDtypeStruct((N, N), F32)] * 2,
        in_specs=[SMEM, VMEM, VMEM, VMEM],
        out_specs=[VMEM, VMEM],
        scratch_shapes=[pltpu.VMEM((N, N), BF16)] * 3,
        compiler_params=pltpu.CompilerParams(vmem_limit_bytes=48 << 20),
        name="prep",
    )(pos, cnt, rs, cs)


def main_body(*refs):
    lt, w, lx = refs[:3]
    left = refs[3:11]
    right = refs[11:13]
    row_out = refs[13:21]
    col_out = refs[21:23]
    rcat, bc, colt = refs[23:]
    for c in range(2):
        for z in range(8):
            at = c * 512 + z * 64
            hi, lo = split(right[c][z * 72 : z * 72 + 64, :])
            rcat[at : at + 64, :D] = hi
            rcat[at : at + 64, D:] = lo
            bc[:, at : at + 64] = right[c][z * 72 + 64 : z * 72 + 65, :64] - lt[0]
    br = jnp.concatenate([left[k][128:129, :128] for k in range(8)], 0).T
    for k in range(4):
        s = slice(256 * k, 256 * (k + 1))
        lv = jnp.concatenate([left[2 * k][:128, :], left[2 * k + 1][:128, :]], 0)
        bv = jnp.concatenate([br[:, 2 * k : 2 * k + 1], br[:, 2 * k + 1 : 2 * k + 2]], 0)
        lh, ll = split(lv)
        score = dot(lh, rcat[:, :D], NT) + dot(lh, rcat[:, D:], NT) + dot(ll, rcat[:, :D], NT)
        d = score + bv + bc[...] - lx[s, :]
        wv = w[s, :]
        g = jnp.where(wv > 0, wv * d, 0.5 * jnp.tanh(0.5 * d) + 0.5)
        gh, gl = split(g)
        rr = dot(gh, rcat[...], NN)
        rr = rr[:, :D] + rr[:, D:] + dot(gl, rcat[:, :D], NN)
        row_out[2 * k][...] = rr[:128]
        row_out[2 * k + 1][...] = rr[128:]
        lt_ = jnp.concatenate([lh, ll], 1).T
        cc = dot(lt_, gh, NN)
        cc = cc[:D] + cc[D:] + dot(lt_[:D], gl, NN)
        if k == 0:
            colt[...] = cc
        else:
            colt[...] += cc
    col = colt[...].T
    col_out[0][...] = col[:512]
    col_out[1][...] = col[512:]


def main(lt, w, lx, left, right):
    return pl.pallas_call(
        main_body,
        out_shape=[jax.ShapeDtypeStruct((128, D), F32)] * 8
        + [jax.ShapeDtypeStruct((512, D), F32)] * 2,
        in_specs=[SMEM] + [VMEM] * 12,
        out_specs=[VMEM] * 10,
        scratch_shapes=[
            pltpu.VMEM((N, 2 * D), BF16),
            pltpu.VMEM((1, N), F32),
            pltpu.VMEM((D, N), F32),
        ],
        compiler_params=pltpu.CompilerParams(vmem_limit_bytes=48 << 20),
        name="main",
    )(lt, w, lx, *left, *right)


def halves_body(own, got, *outs):
    for z in range(8):
        s = slice(64 * z, 64 * z + 64)
        outs[z][...] = own[s, :] + got[s, :]


def halves(own, got):
    return pl.pallas_call(
        halves_body,
        out_shape=[jax.ShapeDtypeStruct((64, D), F32)] * 8,
        in_specs=[VMEM] * 2,
        out_specs=[VMEM] * 8,
        name="halves",
    )(own, got)


def with_logs(embed, marginal):
    logs = jnp.log(marginal.astype(F32))
    return jnp.concatenate([embed, jnp.pad(logs[None], ((0, 7), (0, D - logs.shape[0])))], 0)


def shards(
    tile_counts, row_slot, col_slot, row_embed, col_embed, row_marginal, col_marginal, total_count
):
    log_total = jnp.log(total_count.astype(F32))
    pos = jnp.stack([lax.axis_index("gc"), lax.axis_index("gr")]).astype(jnp.int32)
    own = with_logs(col_embed[0], col_marginal[0])
    other = swap(own, 16)
    pair = jnp.concatenate(
        [own[:32], other[:32], own[32:] + jnp.roll(other[32:], 32, 1)], 0
    )
    rows = with_logs(row_embed[0], row_marginal[0])
    left = [rows] + [shift(rows, "gc", k) for k in range(1, 8)]
    along = jnp.concatenate([pair] + [shift(pair, "gr", k) for k in range(1, 8)], 0)
    right = [along, swap(along, 1)]
    w, lx = prep(pos, tile_counts[0, 0], row_slot[0], col_slot[0])
    outs = main(log_total, w, lx, left, right)
    row_grad = outs[0]
    back = [shift(outs[k], "gc", -k) for k in range(1, 8)]
    pieces = halves(outs[8], swap(outs[9], 1))
    col_pair = pieces[0]
    for k in range(1, 8):
        col_pair = col_pair + shift(pieces[k], "gr", -k)
    for b in back:
        row_grad = row_grad + b
    col_grad = col_pair[:32] + swap(col_pair[32:], 16)
    new_rows = row_embed[0] - 0.001 * row_grad
    new_cols = col_embed[0] - 0.001 * col_grad
    return (new_rows[None], new_cols[None])


def solution(mesh):
    return jax.shard_map(
        shards,
        mesh=mesh,
        in_specs=(
            P("gr", "gc", None, None),
            P("gr", "gc", None),
            P("gr", "gc", None),
            P("gr", "gc", None),
            P("gc", "gr", None),
            P("gr", "gc"),
            P("gc", "gr"),
            P(),
        ),
        out_specs=(P("gr", "gc", None), P("gc", "gr", None)),
        check_vma=False,
    )
```

```python
import jax
import jax.numpy as jnp
from jax import lax
from jax.experimental import pallas as pl
from jax.experimental.pallas import tpu as pltpu
from jax.sharding import PartitionSpec as P

F32 = jnp.float32
BF16 = jnp.bfloat16
N = 1024
D = 256
T = 256
NN = ((1,), (0,))
NT = ((1,), (1,))
VMEM = pl.BlockSpec(memory_space=pltpu.VMEM)
SMEM = pl.BlockSpec(memory_space=pltpu.SMEM)


def f32(*shape):
    return jax.ShapeDtypeStruct(shape, F32)


def bf16(*shape):
    return jax.ShapeDtypeStruct(shape, BF16)


ANY = pl.BlockSpec(memory_space=pl.ANY)
HBM = pl.BlockSpec(memory_space=pltpu.HBM)


def call(body, name, out_shape, operands, smem=0, far=0, after=(), scratch=(), vmem_mb=16, flops=0):
    def run(*refs):
        n = len(operands)
        body(*refs[:n], *refs[n + len(after) :])

    near = len(operands) - smem - far
    operands = [
        pltpu.with_memory_space_constraint(x, pltpu.HBM) if smem <= i < smem + far else x
        for i, x in enumerate(operands)
    ]
    return pl.pallas_call(
        run,
        out_shape=out_shape,
        in_specs=[SMEM] * smem + [HBM] * far + [VMEM] * near + [ANY] * len(after),
        out_specs=[VMEM] * len(out_shape),
        scratch_shapes=list(scratch),
        compiler_params=pltpu.CompilerParams(vmem_limit_bytes=vmem_mb << 20),
        cost_estimate=pl.CostEstimate(flops=flops, bytes_accessed=1 << 16, transcendentals=0),
        name=name,
    )(*operands, *after)


def dot(a, b, dims):
    return lax.dot_general(a, b, (dims, ((), ())), preferred_element_type=F32)


def split(v):
    hi = v.astype(BF16)
    return hi, (v - hi.astype(F32)).astype(BF16)


def move_y(x, k):
    return lax.ppermute(x, "gc", [(i, (i + 2 * k) % 8) for i in range(8)])


def swap_x_hi(x):
    return lax.ppermute(x, "gc", [(i, i ^ 1) for i in range(8)])


def move_z(x, k):
    return lax.ppermute(
        x, "gr", [(i, (i & 17) | (((((i >> 1) & 7) + k) % 8) << 1)) for i in range(32)]
    )


def swap_gr(x, mask):
    return lax.ppermute(x, "gr", [(i, i ^ mask) for i in range(32)])


CORE, Z1, X_LO = 1, 2, 16


def pack_body(total, rows, cols, rm, cm, row_out, col_out, rmv, cmv, sems):
    copies = [
        pltpu.make_async_copy(src, dst, sems.at[i])
        for i, (src, dst) in enumerate(
            [(cols, col_out.at[:32, :]), (cm, cmv), (rows, row_out.at[:128, :]), (rm, rmv)]
        )
    ]
    for c in copies:
        c.start()
    row_out[128:, :] = jnp.zeros((8, D), F32)
    col_out[32:, :] = jnp.zeros((8, D), F32)
    for c in copies:
        c.wait()
    row_out[128:129, :128] = jnp.log(rmv[...].astype(F32))
    log_total = jnp.log(jnp.full((1, 32), total[0], jnp.int32).astype(F32))
    col_out[32:33, :32] = jnp.log(cmv[...].astype(F32)) - log_total


def two_body(a, b, out, *, n, logs):
    out[:n, :] = a[:n, :]
    out[n : 2 * n, :] = b[:n, :]
    out[2 * n :, :] = jnp.zeros((8, D), F32)
    out[2 * n : 2 * n + 1, :128] = a[n : n + 1, :128]
    if logs:
        out[2 * n : 2 * n + 1, logs : 2 * logs] = b[n : n + 1, :logs]
    else:
        out[2 * n + 1 : 2 * n + 2, :128] = b[n : n + 1, :128]


def two(a, b, logs, name, after=()):
    n = a.shape[0] - 8

    def body(*refs):
        two_body(*refs, n=n, logs=logs)

    return call(body, name, [f32(2 * n + 8, D)], [a, b], after=after)[0]


def digits_body(cnt, rs, cs, chi, clo, bt, at, cntv, rsv, csv, sems):
    copies = [pltpu.make_async_copy(rs, rsv, sems.at[0]), pltpu.make_async_copy(cs, csv, sems.at[1])]
    for t in range(4):
        s = pl.ds(T * t, T)
        copies.append(pltpu.make_async_copy(cnt.at[s, :], cntv.at[s, :], sems.at[2 + t]))
    for c in copies:
        c.start()
    gc, gr = lax.axis_index("gc"), lax.axis_index("gr")
    copies[0].wait()
    copies[1].wait()
    rows = rsv[...]
    owner = rows >> 7
    rows = ((((gc >> 1) - (owner >> 1)) & 3) << 8) | (((owner ^ gc) & 1) << 7) | (rows & 127)
    cols = csv[...]
    owner = cols >> 5
    cols = (
        (((owner ^ gr) & 1) << 9)
        | ((((gr >> 2) - (owner >> 2)) & 3) << 7)
        | (((owner ^ gr) & 2) << 5)
        | (((owner ^ gr) & 16) << 1)
        | (cols & 31)
    )
    for t in range(4):
        s = slice(T * t, T * (t + 1))
        j = lax.broadcasted_iota(jnp.int32, (T, N), 0) + t * T
        bt[s, :] = jnp.where(j == cols, 1.0, 0.0).astype(BF16)
        at[s, :] = jnp.where(j == rows, 1.0, 0.0).astype(BF16)
    for t in range(4):
        s = slice(T * t, T * (t + 1))
        copies[2 + t].wait()
        c = cntv[s, :]
        chi[s, :] = (c >> 6).astype(F32).astype(BF16)
        clo[s, :] = (c & 63).astype(F32).astype(BF16)


def order_body(chi, clo, bt, at, w, lx, *, k):
    a = at[T * k : T * (k + 1), :]
    hi = dot(a, chi[...], NN).astype(BF16)
    lo = dot(a, clo[...], NN).astype(BF16)
    x = dot(hi, bt[...], NT) * 64.0 + dot(lo, bt[...], NT)
    w[...] = jnp.where(x > 0, 0.1 + 0.25 * jnp.sqrt(x), 0.0)
    lx[...] = jnp.log(jnp.maximum(x, 1.0))


def half_body(*refs, half, first):
    w, lx, left = refs[:4], refs[4:8], refs[8:12]
    right = refs[12]
    if first:
        gh_out, gl_out, rcat, col_out, lcat, ltr, bvs = refs[13:20]
    else:
        lcat, ltr, bvs = refs[13:16]
        gh_out, gl_out, rcat, col_out = refs[16:20]
    bc, colt = refs[20:]
    for e in range(4):
        at = e * 128
        hi, lo = split(right[e * 136 : e * 136 + 128, :])
        rcat[at : at + 128, :D] = hi
        rcat[at : at + 128, D:] = lo
        bc[:, at : at + 128] = right[e * 136 + 128 : e * 136 + 129, :128]
    h = slice(512 * half, 512 * (half + 1))
    for k in range(4):
        s = slice(T * k, T * (k + 1))
        if first:
            br = left[k][256:264, :128].T
            bvs[s, :] = jnp.concatenate([br[:, 0:1], br[:, 1:2]], 0)
            lh, ll = split(left[k][:256, :])
            lcat[s, :D] = lh
            lcat[s, D:] = ll
            ltr[:, s] = jnp.concatenate([lh, ll], 1).T
        lh, ll = lcat[s, :D], lcat[s, D:]
        score = dot(lh, rcat[:, :D], NT) + dot(lh, rcat[:, D:], NT) + dot(ll, rcat[:, :D], NT)
        d = score + bvs[s, :] + bc[...] - lx[k][:, h]
        wv = w[k][:, h]
        g = jnp.where(wv > 0, wv * d, 0.5 * jnp.tanh(0.5 * d) + 0.5)
        gh, gl = split(g)
        gh_out[s, :] = gh
        gl_out[s, :] = gl
        cc = dot(ltr[:, s], gh, NN)
        cc = cc[:D] + cc[D:] + dot(ltr[:D, s], gl, NN)
        if k == 0:
            colt[...] = cc
        else:
            colt[...] += cc
    col_out[...] = colt[...].T


def rows_body(*refs, first):
    gh, gl, r = refs[:3]
    outs = refs[-4:]
    for k in (2, 1, 3, 0):
        s = slice(T * k, T * (k + 1))
        rr = dot(gh[s, :], r[...], NN)
        rr = rr[:, :D] + rr[:, D:] + dot(gl[s, :], r[:, :D], NN)
        outs[k][...] = rr if first else rr + refs[3 + k][...]


def join_body(*refs):
    for e in range(4):
        refs[4][136 * e : 136 * (e + 1), :] = refs[e][...]


def quarters_body(own, got, *outs):
    for e in range(4):
        s = slice(128 * e, 128 * e + 128)
        outs[e][...] = own[s, :] + got[s, :]


def sum_body(a, b, c, d, keep, give):
    n = keep.shape[0]
    keep[...] = (a[:n, :] + b[:n, :]) + (c[:n, :] + d[:n, :])
    give[...] = (a[n:, :] + b[n:, :]) + (c[n:, :] + d[n:, :])


def add_body(a, b, keep, give):
    n = keep.shape[0]
    keep[...] = a[:n, :] + b[:n, :]
    give[...] = a[n:, :] + b[n:, :]


def last_body(embed, a, b, out):
    out[...] = embed[...] - 0.001 * (a[...] + b[...])


def shards(
    tile_counts, row_slot, col_slot, row_embed, col_embed, row_marginal, col_marginal, total_count
):
    rows, cols = call(
        pack_body,
        "pack",
        [f32(136, D), f32(40, D)],
        [total_count, row_embed[0], col_embed[0], row_marginal, col_marginal],
        smem=1,
        far=4,
        scratch=[
            pltpu.VMEM((1, 128), jnp.int32),
            pltpu.VMEM((1, 32), jnp.int32),
            pltpu.SemaphoreType.DMA((4,)),
        ],
    )
    hot = call(
        digits_body,
        "digits",
        [bf16(N, N)] * 4,
        [tile_counts[0, 0], row_slot[0], col_slot[0]],
        far=3,
        scratch=[
            pltpu.VMEM((N, N), jnp.int32),
            pltpu.VMEM((1, N), jnp.int32),
            pltpu.VMEM((1, N), jnp.int32),
            pltpu.SemaphoreType.DMA((6,)),
        ],
        flops=1 << 30,
    )
    w, lx = [], []

    def order(k, after):
        def body(*refs):
            order_body(*refs, k=k)

        a, b = call(
            body, f"order{k}", [f32(T, N)] * 2, hot, after=after, vmem_mb=24, flops=1 << 31
        )
        w.append(a)
        lx.append(b)

    cols = two(cols, swap_gr(cols, X_LO), 32, "pair_cols", after=hot[:1])
    order(0, [cols])
    rows = two(rows, swap_x_hi(rows), 0, "pair_rows")
    cols = two(cols, swap_gr(cols, Z1), 64, "quad_cols", after=[rows, w[0]])
    for k in range(1, 4):
        order(k, [cols])
    left = [rows] + [move_y(rows, k) for k in range(1, 4)]
    right = call(
        join_body,
        "join",
        [f32(544, D)],
        [cols] + [move_z(cols, 2 * e) for e in range(1, 4)],
        after=left[1:] + w[1:],
    )[0]
    scratch = [pltpu.VMEM((1, 512), F32), pltpu.VMEM((D, 512), F32)]
    half_out = [bf16(N, 512), bf16(N, 512), bf16(512, 2 * D), f32(512, D)]

    def own_body(*refs):
        half_body(*refs, half=0, first=True)

    def other_body(*refs):
        half_body(*refs, half=1, first=False)

    gh1, gl1, r1, col1, lcat, ltr, bvs = call(
        own_body,
        "own",
        half_out + [bf16(N, 2 * D), bf16(2 * D, N), f32(N, 1)],
        [*w, *lx, *left, right],
        scratch=scratch,
        vmem_mb=24,
    )
    gh2, gl2, r2, col2 = call(
        other_body,
        "other",
        half_out,
        [*w, *lx, *left, swap_gr(right, CORE), lcat, ltr, bvs],
        scratch=scratch,
        vmem_mb=24,
    )

    def rows_own(*refs):
        rows_body(*refs, first=True)

    def rows_other(*refs):
        rows_body(*refs, first=False)

    row_own = call(rows_own, "rows_own", [f32(T, D)] * 4, [gh1, gl1, r1], after=[col2], vmem_mb=24)
    parts = call(
        quarters_body, "quarters", [f32(128, D)] * 4, [col1, swap_gr(col2, CORE)], after=row_own[:1]
    )
    outs = call(
        rows_other, "rows_other", [f32(T, D)] * 4, [gh2, gl2, r2, *row_own], after=parts[:1], vmem_mb=24
    )
    row_keep, row_give = call(
        sum_body,
        "sum_rows",
        [f32(128, D)] * 2,
        [outs[0]] + [move_y(outs[k], -k) for k in range(1, 4)],
    )
    col_keep, col_give = call(
        sum_body,
        "sum_cols",
        [f32(64, D)] * 2,
        [parts[0]] + [move_z(parts[e], -2 * e) for e in range(1, 4)],
    )
    col_keep, col_give = call(
        add_body, "add_cols", [f32(32, D)] * 2, [col_keep, swap_gr(col_give, Z1)]
    )
    new_rows = call(
        last_body, "new_rows", [f32(128, D)], [row_embed[0], row_keep, swap_x_hi(row_give)]
    )[0]
    new_cols = call(
        last_body, "new_cols", [f32(32, D)], [col_embed[0], col_keep, swap_gr(col_give, X_LO)]
    )[0]
    return (new_rows[None], new_cols[None])


def solution(mesh):
    return jax.shard_map(
        shards,
        mesh=mesh,
        in_specs=(
            P("gr", "gc", None, None),
            P("gr", "gc", None),
            P("gr", "gc", None),
            P("gr", "gc", None),
            P("gc", "gr", None),
            P("gr", "gc"),
            P("gc", "gr"),
            P(),
        ),
        out_specs=(P("gr", "gc", None), P("gc", "gr", None)),
        check_vma=False,
    )
```

```python
import jax
import jax.numpy as jnp
from jax import lax
from jax.experimental import pallas as pl
from jax.experimental.pallas import tpu as pltpu
from jax.sharding import PartitionSpec as P

F32 = jnp.float32
BF16 = jnp.bfloat16
F8 = jnp.float8_e4m3fn
N = 1024
D = 256
T = 256
NN = ((1,), (0,))
NT = ((1,), (1,))
VMEM = pl.BlockSpec(memory_space=pltpu.VMEM)
SMEM = pl.BlockSpec(memory_space=pltpu.SMEM)


def f32(*shape):
    return jax.ShapeDtypeStruct(shape, F32)


def bf16(*shape):
    return jax.ShapeDtypeStruct(shape, BF16)


ANY = pl.BlockSpec(memory_space=pl.ANY)
HBM = pl.BlockSpec(memory_space=pltpu.HBM)


def call(body, name, out_shape, operands, smem=0, far=0, after=(), scratch=(), vmem_mb=16, flops=0):
    def run(*refs):
        n = len(operands)
        body(*refs[:n], *refs[n + len(after) :])

    near = len(operands) - smem - far
    operands = [
        pltpu.with_memory_space_constraint(x, pltpu.HBM) if smem <= i < smem + far else x
        for i, x in enumerate(operands)
    ]
    return pl.pallas_call(
        run,
        out_shape=out_shape,
        in_specs=[SMEM] * smem + [HBM] * far + [VMEM] * near + [ANY] * len(after),
        out_specs=[VMEM] * len(out_shape),
        scratch_shapes=list(scratch),
        compiler_params=pltpu.CompilerParams(vmem_limit_bytes=vmem_mb << 20),
        cost_estimate=pl.CostEstimate(flops=flops, bytes_accessed=1 << 16, transcendentals=0),
        name=name,
    )(*operands, *after)


def dot(a, b, dims):
    return lax.dot_general(a, b, (dims, ((), ())), preferred_element_type=F32)


def split(v):
    hi = v.astype(BF16)
    return hi, (v - hi.astype(F32)).astype(BF16)


def move_y(x, k):
    return lax.ppermute(x, "gc", [(i, (i + 2 * k) % 8) for i in range(8)])


def swap_x_hi(x):
    return lax.ppermute(x, "gc", [(i, i ^ 1) for i in range(8)])


def move_z(x, k):
    return lax.ppermute(
        x, "gr", [(i, (i & 17) | (((((i >> 1) & 7) + k) % 8) << 1)) for i in range(32)]
    )


def move_z_by_core(x, k):
    return lax.ppermute(
        x,
        "gr",
        [(i, (i & 17) | (((((i >> 1) & 7) + (-k if i & 1 else k)) % 8) << 1)) for i in range(32)],
    )


def swap_gr(x, mask):
    return lax.ppermute(x, "gr", [(i, i ^ mask) for i in range(32)])


CORE, Z1, X_LO = 1, 2, 16
CFG = dict(r1=(1, 2), r2=(3,), y1=0, y2=0, early=1, pr=1, sr=1, qo=1, ro=1, of=31, kf=1 << 33, ownfar=0)


def pack_body(total, rows, cols, rm, cm, row_out, col_out, rmv, cmv, sems):
    copies = [
        pltpu.make_async_copy(src, dst, sems.at[i])
        for i, (src, dst) in enumerate(
            [(cols, col_out.at[:32, :]), (cm, cmv), (rows, row_out.at[:128, :]), (rm, rmv)]
        )
    ]
    for c in copies:
        c.start()
    row_out[128:, :] = jnp.zeros((8, D), F32)
    col_out[32:, :] = jnp.zeros((8, D), F32)
    for c in copies:
        c.wait()
    row_out[128:129, :128] = jnp.log(rmv[...].astype(F32))
    log_total = jnp.log(jnp.full((1, 32), total[0], jnp.int32).astype(F32))
    col_out[32:33, :32] = jnp.log(cmv[...].astype(F32)) - log_total


def two_body(a, b, out, *, n, logs):
    out[:n, :] = a[:n, :]
    out[n : 2 * n, :] = b[:n, :]
    out[2 * n :, :] = jnp.zeros((8, D), F32)
    out[2 * n : 2 * n + 1, :128] = a[n : n + 1, :128]
    if logs:
        out[2 * n : 2 * n + 1, logs : 2 * logs] = b[n : n + 1, :logs]
    else:
        out[2 * n + 1 : 2 * n + 2, :128] = b[n : n + 1, :128]


def two(a, b, logs, name, after=()):
    n = a.shape[0] - 8

    def body(*refs):
        two_body(*refs, n=n, logs=logs)

    return call(body, name, [f32(2 * n + 8, D)], [a, b], after=after)[0]


def digits_body(cnt, rs, cs, c2, c1, c0, bt, at, cntv, rsv, csv, sems):
    copies = [pltpu.make_async_copy(rs, rsv, sems.at[0]), pltpu.make_async_copy(cs, csv, sems.at[1])]
    for t in range(4):
        s = pl.ds(T * t, T)
        copies.append(pltpu.make_async_copy(cnt.at[s, :], cntv.at[s, :], sems.at[2 + t]))
    for c in copies:
        c.start()
    gc, gr = lax.axis_index("gc"), lax.axis_index("gr")
    copies[0].wait()
    copies[1].wait()
    rows = rsv[...]
    owner = rows >> 7
    rows = ((((gc >> 1) - (owner >> 1)) & 3) << 8) | (((owner ^ gc) & 1) << 7) | (rows & 127)
    cols = csv[...]
    owner = cols >> 5
    away = (((gr >> 2) - (owner >> 2)) * (1 - 2 * (gr & 1))) & 3
    cols = (
        ((away ^ (away >> 1)) << 8)
        | (((owner ^ gr) & 1) << 7)
        | (((owner ^ gr) & 2) << 5)
        | (((owner ^ gr) & 16) << 1)
        | (cols & 31)
    )
    for t in range(4):
        s = slice(T * t, T * (t + 1))
        j = lax.broadcasted_iota(jnp.int32, (T, N), 0) + t * T
        bt[s, :] = jnp.where(j == cols, 1.0, 0.0).astype(F8)
        at[s, :] = jnp.where(j == rows, 1.0, 0.0).astype(F8)
    for t in range(4):
        s = slice(T * t, T * (t + 1))
        copies[2 + t].wait()
        c = cntv[s, :]
        c2[s, :] = (c >> 8).astype(F32).astype(F8)
        c1[s, :] = ((c >> 4) & 15).astype(F32).astype(F8)
        c0[s, :] = (c & 15).astype(F32).astype(F8)


def order_body(c2, c1, c0, bt, at, w, lx, *, k):
    a = at[T * k : T * (k + 1), :]
    d2, d1, d0 = (dot(a, c[...], NN).astype(F8) for c in (c2, c1, c0))
    x = dot(d2, bt[...], NT) * 256.0 + dot(d1, bt[...], NT) * 16.0 + dot(d0, bt[...], NT)
    w[...] = jnp.where(x > 0, 0.1 + 0.25 * jnp.sqrt(x), 0.0)
    lx[...] = jnp.log(jnp.maximum(x, 1.0))


def half_body(w, lx, left, right, saved, outs, bc, *, half):
    gh_out, gl_out, rcat = outs
    lcat, ltr, bvs = saved
    for e in range(4):
        at = e * 128
        src, off = right[e]
        hi, lo = split(src[off : off + 128, :])
        rcat[at : at + 128, :D] = hi
        rcat[at : at + 128, D:] = lo
        bc[:, at : at + 128] = src[off + 128 : off + 129, :128]
    h = slice(512 * half, 512 * (half + 1))
    for k in range(4):
        s = slice(T * k, T * (k + 1))
        if half == 0:
            br = left[k][256:264, :128].T
            bvs[s, :] = jnp.concatenate([br[:, 0:1], br[:, 1:2]], 0)
            lh, ll = split(left[k][:256, :])
            lcat[s, :D] = lh
            lcat[s, D:] = ll
            ltr[:, s] = jnp.concatenate([lh, ll], 1).T
        lh, ll = lcat[s, :D], lcat[s, D:]
        score = dot(lh, rcat[:, :D], NT) + dot(lh, rcat[:, D:], NT) + dot(ll, rcat[:, :D], NT)
        d = score + bvs[s, :] + bc[...] - lx[k][:, h]
        wv = w[k][:, h]
        g = jnp.where(wv > 0, wv * d, 0.5 * jnp.tanh(0.5 * d) + 0.5)
        gh, gl = split(g)
        gh_out[s, :] = gh
        gl_out[s, :] = gl
    cc = dot(ltr[...], gh_out[...], NN)
    cc = cc[:D] + cc[D:] + dot(ltr[:D, :], gl_out[...], NN)
    return cc.T


def own_body(*refs):
    w, lx, left = refs[:4], refs[4:8], refs[8:12]
    near, beside, first = refs[12:15]
    gh, gl, rcat, col, lcat, ltr, bvs = refs[15:22]
    (bc,) = refs[22:]
    right = [(near, 0), (beside, 0), (first, 0), (first, 136)]
    col[...] = half_body(w, lx, left, right, (lcat, ltr, bvs), (gh, gl, rcat), bc, half=0)


def other_body(*refs):
    w, lx = refs[:4], refs[4:8]
    second, far, far_beside = refs[8:11]
    saved = refs[11:14]
    col1 = refs[14]
    gh, gl, rcat, keep, give = refs[15:20]
    (bc,) = refs[20:]
    give[:128, :] = col1[128:256, :]
    right = [(second, 136), (second, 0), (far, 0), (far_beside, 0)]
    col = half_body(w, lx, None, right, saved, (gh, gl, rcat), bc, half=1)
    give[256:512, :] = col[:256]
    keep[...] = col[256:384]
    give[128:256, :] = col[384:]


def rows_body(*refs, first):
    gh, gl, r = refs[:3]
    outs = refs[-4:]
    for k in (2, 1, 3, 0):
        s = slice(T * k, T * (k + 1))
        rr = dot(gh[s, :], r[...], NN)
        rr = rr[:, :D] + rr[:, D:] + dot(gl[s, :], r[:, :D], NN)
        outs[k][...] = rr if first else rr + refs[3 + k][...]


def join_body(a, b, out):
    out[:136, :] = a[...]
    out[136:, :] = b[...]


def quarters_body(col1, far, got, near_out, far_out, first_out):
    near_out[...] = col1[:128, :] + got[:128, :]
    far_out[...] = far[...] + got[128:256, :]
    first_out[:128, :] = col1[256:384, :] + got[384:, :]
    first_out[128:, :] = col1[384:, :] + got[256:384, :]


def sum_body(a, b, c, d, keep, give):
    n = keep.shape[0]
    m = 2 * n
    keep[...] = (a[:n, :] + b[:n, :]) + (c[:n, :] + d[:n, :])
    give[...] = (a[n:m, :] + b[n:m, :]) + (c[n:m, :] + d[n:m, :])


def add_body(a, b, keep, give):
    n = keep.shape[0]
    keep[...] = a[:n, :] + b[:n, :]
    give[...] = a[n:, :] + b[n:, :]


def last_body(rows, ra, rb, cols, ca, cb, new_rows, new_cols):
    new_rows[...] = rows[...] - 0.001 * (ra[...] + rb[...])
    new_cols[...] = cols[...] - 0.001 * (ca[...] + cb[...])


def shards(
    tile_counts, row_slot, col_slot, row_embed, col_embed, row_marginal, col_marginal, total_count
):
    rows, cols = call(
        pack_body,
        "pack",
        [f32(136, D), f32(40, D)],
        [total_count, row_embed[0], col_embed[0], row_marginal, col_marginal],
        smem=1,
        far=4,
        scratch=[
            pltpu.VMEM((1, 128), jnp.int32),
            pltpu.VMEM((1, 32), jnp.int32),
            pltpu.SemaphoreType.DMA((4,)),
        ],
    )
    hot = call(
        digits_body,
        "digits",
        [jax.ShapeDtypeStruct((N, N), F8)] * 5,
        [tile_counts[0, 0], row_slot[0], col_slot[0]],
        far=3,
        scratch=[
            pltpu.VMEM((N, N), jnp.int32),
            pltpu.VMEM((1, N), jnp.int32),
            pltpu.VMEM((1, N), jnp.int32),
            pltpu.SemaphoreType.DMA((6,)),
        ],
        flops=1 << CFG["of"],
    )
    w, lx = [], []

    def order(k, after):
        def body(*refs):
            order_body(*refs, k=k)

        a, b = call(
            body, f"order{k}", [f32(T, N)] * 2, hot, after=after, vmem_mb=24, flops=1 << CFG["of"]
        )
        w.append(a)
        lx.append(b)

    cols = two(cols, swap_gr(cols, X_LO), 32, "pair_cols", after=hot[:1])
    order(0, [cols])
    rows = two(rows, swap_x_hi(rows), 0, "pair_rows")
    for k in range(1, CFG["early"]):
        order(k, [cols])
    cols = two(cols, swap_gr(cols, Z1), 64, "quad_cols", after=([rows] if CFG["pr"] else []) + w)
    for k in range(CFG["early"], 4):
        order(k, [cols])
    left = [rows] + [move_y(rows, k) for k in range(1, 4)]
    beside = swap_gr(cols, CORE)
    far = move_z(cols, 4)
    both = call(join_body, "join", [f32(272, D)], [cols, beside])[0]
    first = move_z_by_core(both, 2)

    def relay(x, name, after):
        def body(a, out):
            out[...] = a[...]

        return call(body, name, [f32(*x.shape)], [x], after=after)[0] if after else x

    first = relay(first, "relay_first", [w[k] for k in CFG["r1"]] + left[1:] * CFG["y1"])
    far = relay(far, "relay_far", [w[k] for k in CFG["r2"]] + left[1:] * CFG["y2"])
    second = swap_gr(first, CORE)
    far_beside = swap_gr(far, CORE)

    scratch = [pltpu.VMEM((1, 512), F32)]
    half_out = [bf16(N, 512), bf16(N, 512), bf16(512, 2 * D)]
    gh1, gl1, r1, col1, *saved = call(
        own_body,
        "own",
        half_out + [f32(512, D), bf16(N, 2 * D), bf16(2 * D, N), f32(N, 1)],
        [*w, *lx, *left, cols, beside, first],
        after=[far] * CFG["ownfar"],
        flops=CFG["kf"],
        scratch=scratch,
        vmem_mb=24,
    )
    gh2, gl2, r2, keep, give = call(
        other_body,
        "other",
        half_out + [f32(128, D), f32(512, D)],
        [*w, *lx, second, far, far_beside, *saved, col1],
        flops=CFG["kf"],
        scratch=scratch,
        vmem_mb=24,
    )

    def rows_own(*refs):
        rows_body(*refs, first=True)

    def rows_other(*refs):
        rows_body(*refs, first=False)

    row_own = call(rows_own, "rows_own", [f32(T, D)] * 4, [gh1, gl1, r1], after=[keep], vmem_mb=24)
    near, far, first = call(
        quarters_body,
        "quarters",
        [f32(128, D), f32(128, D), f32(256, D)],
        [col1, keep, swap_gr(give, CORE)],
        after=row_own[: CFG["qo"]],
    )
    outs = call(
        rows_other, "rows_other", [f32(T, D)] * 4, [gh2, gl2, r2, *row_own], after=[near] * CFG["ro"], vmem_mb=24
    )
    far = move_z(far, 4)
    first = move_z_by_core(first, -2)
    second = swap_gr(first[128:], CORE)
    col_keep, col_give = call(
        sum_body, "sum_cols", [f32(64, D)] * 2, [near, far, first, second]
    )
    row_keep, row_give = call(
        sum_body,
        "sum_rows",
        [f32(128, D)] * 2,
        [outs[0]] + [move_y(outs[k], -k) for k in range(1, 4)],
        after=[col_keep] * CFG["sr"],
    )
    col_keep, col_give = call(
        add_body, "add_cols", [f32(32, D)] * 2, [col_keep, swap_gr(col_give, Z1)]
    )
    new_rows, new_cols = call(
        last_body,
        "last",
        [f32(128, D), f32(32, D)],
        [
            row_embed[0],
            row_keep,
            swap_x_hi(row_give),
            col_embed[0],
            col_keep,
            swap_gr(col_give, X_LO),
        ],
    )
    return (new_rows[None], new_cols[None])


def solution(mesh):
    return jax.shard_map(
        shards,
        mesh=mesh,
        in_specs=(
            P("gr", "gc", None, None),
            P("gr", "gc", None),
            P("gr", "gc", None),
            P("gr", "gc", None),
            P("gc", "gr", None),
            P("gr", "gc"),
            P("gc", "gr"),
            P(),
        ),
        out_specs=(P("gr", "gc", None), P("gc", "gr", None)),
        check_vma=False,
    )
```

```python
import jax
import jax.numpy as jnp
from jax import lax
from jax.experimental import pallas as pl
from jax.experimental.pallas import tpu as pltpu
from jax.sharding import PartitionSpec as P

F32 = jnp.float32
BF16 = jnp.bfloat16
F8 = jnp.float8_e4m3fn
N = 1024
D = 256
T = 256
NN = ((1,), (0,))
NT = ((1,), (1,))
VMEM = pl.BlockSpec(memory_space=pltpu.VMEM)
SMEM = pl.BlockSpec(memory_space=pltpu.SMEM)


def f32(*shape):
    return jax.ShapeDtypeStruct(shape, F32)


def bf16(*shape):
    return jax.ShapeDtypeStruct(shape, BF16)


ANY = pl.BlockSpec(memory_space=pl.ANY)
HBM = pl.BlockSpec(memory_space=pltpu.HBM)


def call(body, name, out_shape, operands, smem=0, far=0, after=(), scratch=(), vmem_mb=16, flops=0):
    def run(*refs):
        n = len(operands)
        body(*refs[:n], *refs[n + len(after) :])

    flops = COST.get(name, flops)
    near = len(operands) - smem - far
    operands = [
        pltpu.with_memory_space_constraint(x, pltpu.HBM) if smem <= i < smem + far else x
        for i, x in enumerate(operands)
    ]
    return pl.pallas_call(
        run,
        out_shape=out_shape,
        in_specs=[SMEM] * smem + [HBM] * far + [VMEM] * near + [ANY] * len(after),
        out_specs=[VMEM] * len(out_shape),
        scratch_shapes=list(scratch),
        compiler_params=pltpu.CompilerParams(vmem_limit_bytes=vmem_mb << 20),
        cost_estimate=pl.CostEstimate(flops=flops, bytes_accessed=1 << 16, transcendentals=0),
        name=name,
    )(*operands, *after)


def dot(a, b, dims):
    return lax.dot_general(a, b, (dims, ((), ())), preferred_element_type=F32)


def split(v):
    hi = v.astype(BF16)
    return hi, (v - hi.astype(F32)).astype(BF16)


def move_y(x, k):
    return lax.ppermute(x, "gc", [(i, (i + 2 * k) % 8) for i in range(8)])


def swap_x_hi(x):
    return lax.ppermute(x, "gc", [(i, i ^ 1) for i in range(8)])


def move_z(x, k):
    return lax.ppermute(
        x, "gr", [(i, (i & 17) | (((((i >> 1) & 7) + k) % 8) << 1)) for i in range(32)]
    )


def move_z_by_core(x, k):
    return lax.ppermute(
        x,
        "gr",
        [(i, (i & 17) | (((((i >> 1) & 7) + (-k if i & 1 else k)) % 8) << 1)) for i in range(32)],
    )


def swap_gr(x, mask):
    return lax.ppermute(x, "gr", [(i, i ^ mask) for i in range(32)])


CORE, Z1, X_LO = 1, 2, 16
COST = {'digits': 0, 'order2': 1073741824, 'other': 4294967296, 'rows_other': 1073741824, 'rows': 17179869184, 'quarters': 1073741824, 'arrived': 0, 'pair_rows': 4294967296, 'sum_cols': 134217728}
CFG = {'ao': 0, 'sy': 0, 'r1': (1, 2), 'r2': (3,), 'y1': 1, 'y2': 0, 'early': 1, 'pr': 1, 'sr': 0, 'qo': 1, 'ro': 0, 'of': 31, 'kf': 8589934592, 'ownfar': 0, 'mc': 1, 'rf': 1, 'rz': 0, 'cr': (1,)}


def pack_body(total, rows, cols, rm, cm, row_out, col_out, rmv, cmv, sems):
    copies = [
        pltpu.make_async_copy(src, dst, sems.at[i])
        for i, (src, dst) in enumerate(
            [(cols, col_out.at[:32, :]), (cm, cmv), (rows, row_out.at[:128, :]), (rm, rmv)]
        )
    ]
    for c in copies:
        c.start()
    row_out[128:, :] = jnp.zeros((8, D), F32)
    col_out[32:, :] = jnp.zeros((8, D), F32)
    for c in copies:
        c.wait()
    row_out[128:129, :128] = jnp.log(rmv[...].astype(F32))
    log_total = jnp.log(jnp.full((1, 32), total[0], jnp.int32).astype(F32))
    col_out[32:33, :32] = jnp.log(cmv[...].astype(F32)) - log_total


def two_body(a, b, out, *, n, logs):
    out[:n, :] = a[:n, :]
    out[n : 2 * n, :] = b[:n, :]
    out[2 * n :, :] = jnp.zeros((8, D), F32)
    out[2 * n : 2 * n + 1, :128] = a[n : n + 1, :128]
    if logs:
        out[2 * n : 2 * n + 1, logs : 2 * logs] = b[n : n + 1, :logs]
    else:
        out[2 * n + 1 : 2 * n + 2, :128] = b[n : n + 1, :128]


def two(a, b, logs, name, after=()):
    n = a.shape[0] - 8

    def body(*refs):
        two_body(*refs, n=n, logs=logs)

    return call(body, name, [f32(2 * n + 8, D)], [a, b], after=after)[0]


def digits_body(cnt, rs, cs, c2, c1, c0, bt, at, cntv, rsv, csv, sems):
    copies = [pltpu.make_async_copy(rs, rsv, sems.at[0]), pltpu.make_async_copy(cs, csv, sems.at[1])]
    for t in range(4):
        s = pl.ds(T * t, T)
        copies.append(pltpu.make_async_copy(cnt.at[s, :], cntv.at[s, :], sems.at[2 + t]))
    for c in copies:
        c.start()
    gc, gr = lax.axis_index("gc"), lax.axis_index("gr")
    copies[0].wait()
    copies[1].wait()
    rows = rsv[...]
    owner = rows >> 7
    rows = ((((gc >> 1) - (owner >> 1)) & 3) << 8) | (((owner ^ gc) & 1) << 7) | (rows & 127)
    cols = csv[...]
    owner = cols >> 5
    away = (((gr >> 2) - (owner >> 2)) * (1 - 2 * (gr & 1))) & 3
    cols = (
        ((away ^ (away >> 1)) << 8)
        | (((owner ^ gr) & 1) << 7)
        | (((owner ^ gr) & 2) << 5)
        | (((owner ^ gr) & 16) << 1)
        | (cols & 31)
    )
    for t in range(4):
        s = slice(T * t, T * (t + 1))
        j = lax.broadcasted_iota(jnp.int32, (T, N), 0) + t * T
        bt[s, :] = jnp.where(j == cols, 1.0, 0.0).astype(F8)
        at[s, :] = jnp.where(j == rows, 1.0, 0.0).astype(F8)
    for t in range(4):
        s = slice(T * t, T * (t + 1))
        copies[2 + t].wait()
        c = cntv[s, :]
        c2[s, :] = (c >> 8).astype(F32).astype(F8)
        c1[s, :] = ((c >> 4) & 15).astype(F32).astype(F8)
        c0[s, :] = (c & 15).astype(F32).astype(F8)


def order_body(c2, c1, c0, bt, at, w, lx, *, k):
    a = at[T * k : T * (k + 1), :]
    d2, d1, d0 = (dot(a, c[...], NN).astype(F8) for c in (c2, c1, c0))
    x = dot(d2, bt[...], NT) * 256.0 + dot(d1, bt[...], NT) * 16.0 + dot(d0, bt[...], NT)
    w[...] = jnp.where(x > 0, 0.1 + 0.25 * jnp.sqrt(x), 0.0)
    lx[...] = jnp.log(jnp.maximum(x, 1.0))


def half_body(w, lx, left, right, saved, outs, bc, *, half):
    gh_out, gl_out, rcat = outs
    lcat, ltr, bvs = saved
    for e in range(4):
        at = e * 128
        src, off = right[e]
        hi, lo = split(src[off : off + 128, :])
        rcat[at : at + 128, :D] = hi
        rcat[at : at + 128, D:] = lo
        bc[:, at : at + 128] = src[off + 128 : off + 129, :128]
    h = slice(512 * half, 512 * (half + 1))
    for k in range(4):
        s = slice(T * k, T * (k + 1))
        if half == 0:
            br = left[k][256:264, :128].T
            bvs[s, :] = jnp.concatenate([br[:, 0:1], br[:, 1:2]], 0)
            lh, ll = split(left[k][:256, :])
            lcat[s, :D] = lh
            lcat[s, D:] = ll
            ltr[:, s] = jnp.concatenate([lh, ll], 1).T
        lh, ll = lcat[s, :D], lcat[s, D:]
        score = dot(lh, rcat[:, :D], NT) + dot(lh, rcat[:, D:], NT) + dot(ll, rcat[:, :D], NT)
        d = score + bvs[s, :] + bc[...] - lx[k][:, h]
        wv = w[k][:, h]
        g = jnp.where(wv > 0, wv * d, 0.5 * jnp.tanh(0.5 * d) + 0.5)
        gh, gl = split(g)
        gh_out[s, :] = gh
        gl_out[s, :] = gl
    cc = dot(ltr[...], gh_out[...], NN)
    cc = cc[:D] + cc[D:] + dot(ltr[:D, :], gl_out[...], NN)
    return cc.T


def own_body(*refs):
    w, lx, left = refs[:4], refs[4:8], refs[8:12]
    near, beside, first = refs[12:15]
    gh, gl, rcat, col, lcat, ltr, bvs = refs[15:22]
    (bc,) = refs[22:]
    right = [(near, 0), (beside, 0), (first, 0), (first, 136)]
    col[...] = half_body(w, lx, left, right, (lcat, ltr, bvs), (gh, gl, rcat), bc, half=0)


def other_body(sums, right, *refs):
    saved = refs[:3]
    col1 = refs[3]
    gh, gl, rcat, keep, give, bc = refs[4:]
    give[:128, :] = col1[128:256, :]
    col = half_body(sums[:4], sums[4:], None, right, saved, (gh, gl, rcat), bc, half=1)
    give[256:512, :] = col[:256]
    keep[...] = col[256:384]
    give[128:256, :] = col[384:]


def rows_body(*refs, first):
    gh, gl, r = refs[:3]
    outs = refs[-4:]
    for k in (2, 1, 3, 0):
        s = slice(T * k, T * (k + 1))
        rr = dot(gh[s, :], r[...], NN)
        rr = rr[:, :D] + rr[:, D:] + dot(gl[s, :], r[:, :D], NN)
        outs[k][...] = rr if first else rr + refs[3 + k][...]


def join_body(a, b, out):
    out[:136, :] = a[...]
    out[136:, :] = b[...]


def quarters_body(col1, far, got, near_out, far_out, first_out):
    near_out[...] = col1[:128, :] + got[:128, :]
    far_out[...] = far[...] + got[128:256, :]
    first_out[:128, :] = col1[256:384, :] + got[384:, :]
    first_out[128:, :] = col1[384:, :] + got[256:384, :]


def sum_body(*refs):
    *terms, keep, give = refs
    n = keep.shape[0]
    for out, at in ((keep, 0), (give, n)):
        total = terms[0][at : at + n, :]
        for t in terms[1:]:
            total = total + t[at : at + n, :]
        out[...] = total


def fold_body(one, low, three, high, down, up):
    down[:128, :] = one[:128, :] + low[...]
    down[128:, :] = one[128:, :]
    up[:128, :] = three[:128, :]
    up[128:, :] = three[128:, :] + high[...]


def add_body(a, b, keep, give):
    n = keep.shape[0]
    keep[...] = a[:n, :] + b[:n, :]
    give[...] = a[n:, :] + b[n:, :]


def last_body(rows, ra, rb, cols, ca, cb, new_rows, new_cols):
    new_rows[...] = rows[...] - 0.001 * (ra[...] + rb[...])
    new_cols[...] = cols[...] - 0.001 * (ca[...] + cb[...])


def shards(
    tile_counts, row_slot, col_slot, row_embed, col_embed, row_marginal, col_marginal, total_count
):
    rows, cols = call(
        pack_body,
        "pack",
        [f32(136, D), f32(40, D)],
        [total_count, row_embed[0], col_embed[0], row_marginal, col_marginal],
        smem=1,
        far=4,
        scratch=[
            pltpu.VMEM((1, 128), jnp.int32),
            pltpu.VMEM((1, 32), jnp.int32),
            pltpu.SemaphoreType.DMA((4,)),
        ],
    )
    hot = call(
        digits_body,
        "digits",
        [jax.ShapeDtypeStruct((N, N), F8)] * 5,
        [tile_counts[0, 0], row_slot[0], col_slot[0]],
        far=3,
        scratch=[
            pltpu.VMEM((N, N), jnp.int32),
            pltpu.VMEM((1, N), jnp.int32),
            pltpu.VMEM((1, N), jnp.int32),
            pltpu.SemaphoreType.DMA((6,)),
        ],
        flops=1 << CFG["of"],
    )
    w, lx = [], []

    def order(k, after):
        def body(*refs):
            order_body(*refs, k=k)

        a, b = call(
            body, f"order{k}", [f32(T, N)] * 2, hot, after=after, vmem_mb=24, flops=1 << CFG["of"]
        )
        w.append(a)
        lx.append(b)

    cols = two(cols, swap_gr(cols, X_LO), 32, "pair_cols", after=hot[:1])
    order(0, [cols])
    rows = two(rows, swap_x_hi(rows), 0, "pair_rows")
    for k in range(1, CFG["early"]):
        order(k, [cols])
    cols = two(cols, swap_gr(cols, Z1), 64, "quad_cols", after=([rows] if CFG["pr"] else []) + w)
    for k in range(CFG["early"], 4):
        order(k, [cols])
    left = [rows] + [move_y(rows, k) for k in range(1, 4)]
    beside = swap_gr(cols, CORE)
    far = move_z(cols, 4)
    both = call(join_body, "join", [f32(272, D)], [cols, beside])[0]
    first = move_z_by_core(both, 2)

    def relay(name, parts, after):
        def body(*refs):
            at = 0
            for p in refs[:-1]:
                refs[-1][at : at + p.shape[0], :] = p[...]
                at += p.shape[0]

        rows = sum(p.shape[0] for p in parts)
        return call(body, name, [f32(rows, D)], parts, after=after)[0]

    def other_run(*refs):
        n = 8 + len(crossed)
        right = [(refs[8 + i], at) for i, at in spots]
        other_body(refs[:8], right, *refs[n:])

    scratch = [pltpu.VMEM((1, 512), F32)]
    half_out = [bf16(N, 512), bf16(N, 512), bf16(512, 2 * D)]
    gh1, gl1, r1, col1, *saved = call(
        own_body,
        "own",
        half_out + [f32(512, D), bf16(N, 2 * D), bf16(2 * D, N), f32(N, 1)],
        [*w, *lx, *left, cols, beside, first],
        after=[far] * CFG["ownfar"],
        flops=CFG["kf"],
        scratch=scratch,
        vmem_mb=24,
    )
    if CFG["mc"]:
        give = relay("arrived", [first, far], [w[k] for k in CFG["cr"]] + left[1:] * CFG["y1"] + [gh1] * CFG["ao"])
        second = swap_gr(give, CORE)
        crossed = [second, far]
        spots = [(0, 136), (0, 0), (1, 0), (0, 272)]
    else:
        first = relay("relay_first", [first], [w[k] for k in CFG["r1"]] + left[1:] * CFG["y1"])
        far = relay("relay_far", [far], [w[k] for k in CFG["r2"]] + left[1:] * CFG["y2"])
        crossed = [swap_gr(first, CORE), far, swap_gr(far, CORE)]
        spots = [(0, 136), (0, 0), (1, 0), (2, 0)]

    gh2, gl2, r2, keep, give = call(
        other_run,
        "other",
        half_out + [f32(128, D), f32(512, D)],
        [*w, *lx, *crossed, *saved, col1],
        flops=CFG["kf"],
        scratch=scratch,
        vmem_mb=24,
    )

    def rows_own(*refs):
        rows_body(*refs, first=True)

    def rows_other(*refs):
        rows_body(*refs, first=False)

    def rows_all(*refs):
        outs = refs[-4:]
        for k in (2, 1, 3, 0):
            s = slice(T * k, T * (k + 1))
            total = 0.0
            for gh, gl, r in (refs[:3], refs[3:6]):
                rr = dot(gh[s, :], r[...], NN)
                total += rr[:, :D] + rr[:, D:] + dot(gl[s, :], r[:, :D], NN)
            outs[k][...] = total

    if CFG["rf"]:
        row_own = outs = call(
            rows_all, "rows", [f32(T, D)] * 4, [gh1, gl1, r1, gh2, gl2, r2], vmem_mb=24
        )
    else:
        row_own = call(
            rows_own, "rows_own", [f32(T, D)] * 4, [gh1, gl1, r1], after=[keep], vmem_mb=24
        )
    near, far, first = call(
        quarters_body,
        "quarters",
        [f32(128, D), f32(128, D), f32(256, D)],
        [col1, keep, swap_gr(give, CORE)],
        after=row_own[: CFG["qo"]],
    )
    if not CFG["rf"]:
        outs = call(
            rows_other,
            "rows_other",
            [f32(T, D)] * 4,
            [gh2, gl2, r2, *row_own],
            after=[near] * CFG["ro"],
            vmem_mb=24,
        )
    far = move_z(far, 4)
    first = move_z_by_core(first, -2)
    second = first[128:]
    if CFG["rz"]:
        second = relay("relay_far_sum", [second], [far])
    second = swap_gr(second, CORE)
    col_keep, col_give = call(
        sum_body, "sum_cols", [f32(64, D)] * 2, [near, far, first, second]
    )
    if CFG["sy"]:
        low = move_y(outs[2][:128], -1)
        high = move_y(outs[2][128:], 1)
        down, up = call(fold_body, "fold", [f32(T, D)] * 2, [outs[1], low, outs[3], high])
        row_terms = [outs[0], move_y(down, -1), move_y(up, 1)]
    else:
        row_terms = [outs[0]] + [move_y(outs[k], -k) for k in range(1, 4)]
    row_keep, row_give = call(
        sum_body, "sum_rows", [f32(128, D)] * 2, row_terms, after=[col_keep] * CFG["sr"]
    )
    col_keep, col_give = call(
        add_body, "add_cols", [f32(32, D)] * 2, [col_keep, swap_gr(col_give, Z1)]
    )
    new_rows, new_cols = call(
        last_body,
        "last",
        [f32(128, D), f32(32, D)],
        [
            row_embed[0],
            row_keep,
            swap_x_hi(row_give),
            col_embed[0],
            col_keep,
            swap_gr(col_give, X_LO),
        ],
    )
    return (new_rows[None], new_cols[None])


def solution(mesh):
    return jax.shard_map(
        shards,
        mesh=mesh,
        in_specs=(
            P("gr", "gc", None, None),
            P("gr", "gc", None),
            P("gr", "gc", None),
            P("gr", "gc", None),
            P("gc", "gr", None),
            P("gr", "gc"),
            P("gc", "gr"),
            P(),
        ),
        out_specs=(P("gr", "gc", None), P("gc", "gr", None)),
        check_vma=False,
    )
```

```python
import jax
import jax.numpy as jnp
from jax import lax
from jax.experimental import pallas as pl
from jax.experimental.pallas import tpu as pltpu
from jax.sharding import PartitionSpec as P

F32 = jnp.float32
BF16 = jnp.bfloat16
F8 = jnp.float8_e4m3fn
N = 1024
D = 256
T = 256
NN = ((1,), (0,))
NT = ((1,), (1,))
VMEM = pl.BlockSpec(memory_space=pltpu.VMEM)
SMEM = pl.BlockSpec(memory_space=pltpu.SMEM)


def f32(*shape):
    return jax.ShapeDtypeStruct(shape, F32)


def bf16(*shape):
    return jax.ShapeDtypeStruct(shape, BF16)


ANY = pl.BlockSpec(memory_space=pl.ANY)
HBM = pl.BlockSpec(memory_space=pltpu.HBM)


def call(body, name, out_shape, operands, smem=0, far=0, after=(), scratch=(), vmem_mb=16, flops=0):
    def run(*refs):
        n = len(operands)
        body(*refs[:n], *refs[n + len(after) :])

    flops = COST.get(name, flops)
    near = len(operands) - smem - far
    operands = [
        pltpu.with_memory_space_constraint(x, pltpu.HBM) if smem <= i < smem + far else x
        for i, x in enumerate(operands)
    ]
    return pl.pallas_call(
        run,
        out_shape=out_shape,
        in_specs=[SMEM] * smem + [HBM] * far + [VMEM] * near + [ANY] * len(after),
        out_specs=[VMEM] * len(out_shape),
        scratch_shapes=list(scratch),
        compiler_params=pltpu.CompilerParams(vmem_limit_bytes=vmem_mb << 20),
        cost_estimate=pl.CostEstimate(flops=flops, bytes_accessed=1 << 16, transcendentals=0),
        name=name,
    )(*operands, *after)


def dot(a, b, dims):
    return lax.dot_general(a, b, (dims, ((), ())), preferred_element_type=F32)


def split(v):
    hi = v.astype(BF16)
    return hi, (v - hi.astype(F32)).astype(BF16)


def move_y(x, k):
    return lax.ppermute(x, "gc", [(i, (i + 2 * k) % 8) for i in range(8)])


def swap_x_hi(x):
    return lax.ppermute(x, "gc", [(i, i ^ 1) for i in range(8)])


def move_z(x, k):
    return lax.ppermute(
        x, "gr", [(i, (i & 17) | (((((i >> 1) & 7) + k) % 8) << 1)) for i in range(32)]
    )


def move_z_by_core(x, k):
    return lax.ppermute(
        x,
        "gr",
        [(i, (i & 17) | (((((i >> 1) & 7) + (-k if i & 1 else k)) % 8) << 1)) for i in range(32)],
    )


def swap_gr(x, mask):
    return lax.ppermute(x, "gr", [(i, i ^ mask) for i in range(32)])


CORE, Z1, X_LO = 1, 2, 16
COST = {'digits': 0, 'order2': 1073741824, 'other': 4294967296, 'rows_other': 1073741824, 'rows': 17179869184, 'quarters': 1073741824, 'arrived': 0, 'pair_rows': 4294967296, 'sum_cols': 134217728}
CFG = {'ao': 0, 'sy': 0, 'r1': (1, 2), 'r2': (3,), 'y1': 1, 'y2': 0, 'early': 1, 'pr': 1, 'sr': 0, 'qo': 1, 'ro': 0, 'of': 31, 'kf': 8589934592, 'ownfar': 0, 'mc': 1, 'rf': 1, 'rz': 0, 'cr': (1,)}


def pack_body(total, rows, cols, rm, cm, row_out, col_out, rmv, cmv, sems):
    copies = [
        pltpu.make_async_copy(src, dst, sems.at[i])
        for i, (src, dst) in enumerate(
            [(cols, col_out.at[:32, :]), (cm, cmv), (rows, row_out.at[:128, :]), (rm, rmv)]
        )
    ]
    for c in copies:
        c.start()
    row_out[128:, :] = jnp.zeros((8, D), F32)
    col_out[32:, :] = jnp.zeros((8, D), F32)
    for c in copies:
        c.wait()
    row_out[128:129, :128] = jnp.log(rmv[...].astype(F32))
    log_total = jnp.log(jnp.full((1, 32), total[0], jnp.int32).astype(F32))
    col_out[32:33, :32] = jnp.log(cmv[...].astype(F32)) - log_total


def two_body(a, b, out, *, n, logs):
    out[:n, :] = a[:n, :]
    out[n : 2 * n, :] = b[:n, :]
    out[2 * n :, :] = jnp.zeros((8, D), F32)
    out[2 * n : 2 * n + 1, :128] = a[n : n + 1, :128]
    if logs:
        out[2 * n : 2 * n + 1, logs : 2 * logs] = b[n : n + 1, :logs]
    else:
        out[2 * n + 1 : 2 * n + 2, :128] = b[n : n + 1, :128]


def two(a, b, logs, name, after=()):
    n = a.shape[0] - 8

    def body(*refs):
        two_body(*refs, n=n, logs=logs)

    return call(body, name, [f32(2 * n + 8, D)], [a, b], after=after)[0]


def digits_body(cnt, rs, cs, c2, c1, c0, bt, at, cntv, rsv, csv, sems):
    copies = [pltpu.make_async_copy(rs, rsv, sems.at[0]), pltpu.make_async_copy(cs, csv, sems.at[1])]
    for t in range(4):
        s = pl.ds(T * t, T)
        copies.append(pltpu.make_async_copy(cnt.at[s, :], cntv.at[s, :], sems.at[2 + t]))
    for c in copies:
        c.start()
    gc, gr = lax.axis_index("gc"), lax.axis_index("gr")
    copies[0].wait()
    copies[1].wait()
    rows = rsv[...]
    owner = rows >> 7
    rows = ((((gc >> 1) - (owner >> 1)) & 3) << 8) | (((owner ^ gc) & 1) << 7) | (rows & 127)
    cols = csv[...]
    owner = cols >> 5
    away = (((gr >> 2) - (owner >> 2)) * (1 - 2 * (gr & 1))) & 3
    cols = (
        ((away ^ (away >> 1)) << 8)
        | (((owner ^ gr) & 1) << 7)
        | (((owner ^ gr) & 2) << 5)
        | (((owner ^ gr) & 16) << 1)
        | (cols & 31)
    )
    for t in range(4):
        s = slice(T * t, T * (t + 1))
        j = lax.broadcasted_iota(jnp.int32, (T, N), 0) + t * T
        bt[s, :] = jnp.where(j == cols, 1.0, 0.0).astype(F8)
        at[s, :] = jnp.where(j == rows, 1.0, 0.0).astype(F8)
    for t in range(4):
        s = slice(T * t, T * (t + 1))
        copies[2 + t].wait()
        c = cntv[s, :]
        c2[s, :] = (c >> 8).astype(F32).astype(F8)
        c1[s, :] = ((c >> 4) & 15).astype(F32).astype(F8)
        c0[s, :] = (c & 15).astype(F32).astype(F8)


def order_body(c2, c1, c0, bt, at, w, lx, *, k):
    a = at[T * k : T * (k + 1), :]
    d2, d1, d0 = (dot(a, c[...], NN).astype(F8) for c in (c2, c1, c0))
    x = dot(d2, bt[...], NT) * 256.0 + dot(d1, bt[...], NT) * 16.0 + dot(d0, bt[...], NT)
    w[...] = jnp.where(x > 0, 0.1 + 0.25 * jnp.sqrt(x), 0.0)
    lx[...] = jnp.log(jnp.maximum(x, 1.0))


def half_body(w, lx, left, right, saved, outs, bc, *, half):
    gh_out, gl_out, rcat = outs
    lcat, ltr, bvs = saved
    for e in range(4):
        at = e * 128
        src, off = right[e]
        hi, lo = split(src[off : off + 128, :])
        rcat[at : at + 128, :D] = hi
        rcat[at : at + 128, D:] = lo
        bc[:, at : at + 128] = src[off + 128 : off + 129, :128]
    h = slice(512 * half, 512 * (half + 1))
    for k in range(4):
        s = slice(T * k, T * (k + 1))
        lh, ll = lcat[s, :D], lcat[s, D:]
        score = dot(lh, rcat[:, :D], NT) + dot(lh, rcat[:, D:], NT) + dot(ll, rcat[:, :D], NT)
        d = score + bvs[s, :] + bc[...] - lx[k][:, h]
        wv = w[k][:, h]
        g = jnp.where(wv > 0, wv * d, 0.5 * jnp.tanh(0.5 * d) + 0.5)
        gh, gl = split(g)
        gh_out[s, :] = gh
        gl_out[s, :] = gl
    cc = dot(ltr[...], gh_out[...], NN)
    cc = cc[:D] + cc[D:] + dot(ltr[:D, :], gl_out[...], NN)
    return cc.T


def lefts_body(*refs):
    left, (lcat, ltr, bvs) = refs[:4], refs[4:]
    for k in range(4):
        s = slice(T * k, T * (k + 1))
        br = left[k][256:264, :128].T
        bvs[s, :] = jnp.concatenate([br[:, 0:1], br[:, 1:2]], 0)
        lh, ll = split(left[k][:256, :])
        lcat[s, :D] = lh
        lcat[s, D:] = ll
        ltr[:, s] = jnp.concatenate([lh, ll], 1).T


def own_body(*refs):
    w, lx, saved = refs[:4], refs[4:8], refs[8:11]
    near, beside, first = refs[11:14]
    gh, gl, rcat, col = refs[14:18]
    (bc,) = refs[18:]
    right = [(near, 0), (beside, 0), (first, 0), (first, 136)]
    col[...] = half_body(w, lx, None, right, saved, (gh, gl, rcat), bc, half=0)


def other_body(sums, right, *refs):
    saved = refs[:3]
    col1 = refs[3]
    gh, gl, rcat, keep, give, bc = refs[4:]
    give[:128, :] = col1[128:256, :]
    col = half_body(sums[:4], sums[4:], None, right, saved, (gh, gl, rcat), bc, half=1)
    give[256:512, :] = col[:256]
    keep[...] = col[256:384]
    give[128:256, :] = col[384:]


def rows_body(*refs, first):
    gh, gl, r = refs[:3]
    outs = refs[-4:]
    for k in (2, 1, 3, 0):
        s = slice(T * k, T * (k + 1))
        rr = dot(gh[s, :], r[...], NN)
        rr = rr[:, :D] + rr[:, D:] + dot(gl[s, :], r[:, :D], NN)
        outs[k][...] = rr if first else rr + refs[3 + k][...]


def join_body(a, b, out):
    out[:136, :] = a[...]
    out[136:, :] = b[...]


def quarters_body(col1, far, got, near_out, far_out, first_out):
    near_out[...] = col1[:128, :] + got[:128, :]
    far_out[...] = far[...] + got[128:256, :]
    first_out[:128, :] = col1[256:384, :] + got[384:, :]
    first_out[128:, :] = col1[384:, :] + got[256:384, :]


def sum_body(*refs):
    *terms, keep, give = refs
    n = keep.shape[0]
    for out, at in ((keep, 0), (give, n)):
        total = terms[0][at : at + n, :]
        for t in terms[1:]:
            total = total + t[at : at + n, :]
        out[...] = total


def fold_body(one, low, three, high, down, up):
    down[:128, :] = one[:128, :] + low[...]
    down[128:, :] = one[128:, :]
    up[:128, :] = three[:128, :]
    up[128:, :] = three[128:, :] + high[...]


def add_body(a, b, keep, give):
    n = keep.shape[0]
    keep[...] = a[:n, :] + b[:n, :]
    give[...] = a[n:, :] + b[n:, :]


def last_body(rows, ra, rb, cols, ca, cb, new_rows, new_cols):
    new_rows[...] = rows[...] - 0.001 * (ra[...] + rb[...])
    new_cols[...] = cols[...] - 0.001 * (ca[...] + cb[...])


def shards(
    tile_counts, row_slot, col_slot, row_embed, col_embed, row_marginal, col_marginal, total_count
):
    rows, cols = call(
        pack_body,
        "pack",
        [f32(136, D), f32(40, D)],
        [total_count, row_embed[0], col_embed[0], row_marginal, col_marginal],
        smem=1,
        far=4,
        scratch=[
            pltpu.VMEM((1, 128), jnp.int32),
            pltpu.VMEM((1, 32), jnp.int32),
            pltpu.SemaphoreType.DMA((4,)),
        ],
    )
    hot = call(
        digits_body,
        "digits",
        [jax.ShapeDtypeStruct((N, N), F8)] * 5,
        [tile_counts[0, 0], row_slot[0], col_slot[0]],
        far=3,
        scratch=[
            pltpu.VMEM((N, N), jnp.int32),
            pltpu.VMEM((1, N), jnp.int32),
            pltpu.VMEM((1, N), jnp.int32),
            pltpu.SemaphoreType.DMA((6,)),
        ],
        flops=1 << CFG["of"],
    )
    w, lx = [], []

    def order(k, after):
        def body(*refs):
            order_body(*refs, k=k)

        a, b = call(
            body, f"order{k}", [f32(T, N)] * 2, hot, after=after, vmem_mb=24, flops=1 << CFG["of"]
        )
        w.append(a)
        lx.append(b)

    cols = two(cols, swap_gr(cols, X_LO), 32, "pair_cols", after=hot[:1])
    order(0, [cols])
    rows = two(rows, swap_x_hi(rows), 0, "pair_rows")
    for k in range(1, CFG["early"]):
        order(k, [cols])
    cols = two(cols, swap_gr(cols, Z1), 64, "quad_cols", after=([rows] if CFG["pr"] else []) + w)
    for k in range(CFG["early"], 4):
        order(k, [cols])
    left = [rows] + [move_y(rows, k) for k in range(1, 4)]
    beside = swap_gr(cols, CORE)
    far = move_z(cols, 4)
    both = call(join_body, "join", [f32(272, D)], [cols, beside])[0]
    first = move_z_by_core(both, 2)

    def relay(name, parts, after):
        def body(*refs):
            at = 0
            for p in refs[:-1]:
                refs[-1][at : at + p.shape[0], :] = p[...]
                at += p.shape[0]

        rows = sum(p.shape[0] for p in parts)
        return call(body, name, [f32(rows, D)], parts, after=after)[0]

    def other_run(*refs):
        n = 8 + len(crossed)
        right = [(refs[8 + i], at) for i, at in spots]
        other_body(refs[:8], right, *refs[n:])

    scratch = [pltpu.VMEM((1, 512), F32)]
    half_out = [bf16(N, 512), bf16(N, 512), bf16(512, 2 * D)]
    saved = call(
        lefts_body, "lefts", [bf16(N, 2 * D), bf16(2 * D, N), f32(N, 1)], left, vmem_mb=24
    )
    gh1, gl1, r1, col1 = call(
        own_body,
        "own",
        half_out + [f32(512, D)],
        [*w, *lx, *saved, cols, beside, first],
        after=[far] * CFG["ownfar"],
        flops=CFG["kf"],
        scratch=scratch,
        vmem_mb=24,
    )
    if CFG["mc"]:
        give = relay("arrived", [first, far], [w[k] for k in CFG["cr"]] + left[1:] * CFG["y1"] + [saved[0]])
        second = swap_gr(give, CORE)
        crossed = [second, far]
        spots = [(0, 136), (0, 0), (1, 0), (0, 272)]
    else:
        first = relay("relay_first", [first], [w[k] for k in CFG["r1"]] + left[1:] * CFG["y1"])
        far = relay("relay_far", [far], [w[k] for k in CFG["r2"]] + left[1:] * CFG["y2"])
        crossed = [swap_gr(first, CORE), far, swap_gr(far, CORE)]
        spots = [(0, 136), (0, 0), (1, 0), (2, 0)]

    gh2, gl2, r2, keep, give = call(
        other_run,
        "other",
        half_out + [f32(128, D), f32(512, D)],
        [*w, *lx, *crossed, *saved, col1],
        flops=CFG["kf"],
        scratch=scratch,
        vmem_mb=24,
    )

    def rows_own(*refs):
        rows_body(*refs, first=True)

    def rows_other(*refs):
        rows_body(*refs, first=False)

    def rows_all(*refs):
        outs = refs[-4:]
        for k in (2, 1, 3, 0):
            s = slice(T * k, T * (k + 1))
            total = 0.0
            for gh, gl, r in (refs[:3], refs[3:6]):
                rr = dot(gh[s, :], r[...], NN)
                total += rr[:, :D] + rr[:, D:] + dot(gl[s, :], r[:, :D], NN)
            outs[k][...] = total

    if CFG["rf"]:
        row_own = outs = call(
            rows_all, "rows", [f32(T, D)] * 4, [gh1, gl1, r1, gh2, gl2, r2], vmem_mb=24
        )
    else:
        row_own = call(
            rows_own, "rows_own", [f32(T, D)] * 4, [gh1, gl1, r1], after=[keep], vmem_mb=24
        )
    near, far, first = call(
        quarters_body,
        "quarters",
        [f32(128, D), f32(128, D), f32(256, D)],
        [col1, keep, swap_gr(give, CORE)],
        after=row_own[: CFG["qo"]],
    )
    if not CFG["rf"]:
        outs = call(
            rows_other,
            "rows_other",
            [f32(T, D)] * 4,
            [gh2, gl2, r2, *row_own],
            after=[near] * CFG["ro"],
            vmem_mb=24,
        )
    far = move_z(far, 4)
    first = move_z_by_core(first, -2)
    second = first[128:]
    if CFG["rz"]:
        second = relay("relay_far_sum", [second], [far])
    second = swap_gr(second, CORE)
    col_keep, col_give = call(
        sum_body, "sum_cols", [f32(64, D)] * 2, [near, far, first, second]
    )
    if CFG["sy"]:
        low = move_y(outs[2][:128], -1)
        high = move_y(outs[2][128:], 1)
        down, up = call(fold_body, "fold", [f32(T, D)] * 2, [outs[1], low, outs[3], high])
        row_terms = [outs[0], move_y(down, -1), move_y(up, 1)]
    else:
        row_terms = [outs[0]] + [move_y(outs[k], -k) for k in range(1, 4)]
    row_keep, row_give = call(
        sum_body, "sum_rows", [f32(128, D)] * 2, row_terms, after=[col_keep] * CFG["sr"]
    )
    col_keep, col_give = call(
        add_body, "add_cols", [f32(32, D)] * 2, [col_keep, swap_gr(col_give, Z1)]
    )
    new_rows, new_cols = call(
        last_body,
        "last",
        [f32(128, D), f32(32, D)],
        [
            row_embed[0],
            row_keep,
            swap_x_hi(row_give),
            col_embed[0],
            col_keep,
            swap_gr(col_give, X_LO),
        ],
    )
    return (new_rows[None], new_cols[None])


def solution(mesh):
    return jax.shard_map(
        shards,
        mesh=mesh,
        in_specs=(
            P("gr", "gc", None, None),
            P("gr", "gc", None),
            P("gr", "gc", None),
            P("gr", "gc", None),
            P("gc", "gr", None),
            P("gr", "gc"),
            P("gc", "gr"),
            P(),
        ),
        out_specs=(P("gr", "gc", None), P("gc", "gr", None)),
        check_vma=False,
    )
```
